32 devices in a mesh: row: 8 (over z, core), col: 4 (over y, x).
Axes of the slice: x: 2, y: 2, z: 4, core: 2. Of those that a mesh axis runs over, the one named last changes fastest.
Arguments:
- tokens: bfloat16 [512, 12288], P('col', 'row'), may hold values from -6 to 6
- weight_in: bfloat16 [12288, 24576], P('row', 'col'), may hold values from -0.0546875 to 0.0546875
- weight_out: bfloat16 [24576, 12288], P('col', 'row'), may hold values from -0.0390625 to 0.0390625
- bias_in: bfloat16 [24576], P('col'), may hold values from -3 to 3
- cotangent: bfloat16 [512, 12288], P('col', 'row'), may hold values from -6 to 6
Outputs:
- output: bfloat16 [512, 12288], P('col', 'row')
- grad_tokens: bfloat16 [512, 12288], P('col', 'row')
- grad_weight_in: bfloat16 [12288, 24576], P('row', 'col')
- grad_weight_out: bfloat16 [24576, 12288], P('col', 'row')
- grad_bias: float32 [24576], P('col')
The draws below stay inside these ranges and needn't reach their ends.
All inputs are finite; a program needn't handle non-finite values.
Results may differ from the reference program's by a relative error of at most 0.03.
Values may be sent and summed in bfloat16 or wider, within the bound.
A program may use at most 192 MiB of HBM per device.

```python
import math
import jax
import jax.numpy as jnp
from jax import lax

D = 12288
FF = 24576
TOKENS = 512
N_ROW = 8
N_COL = 4


def steps_of(own_key, extent, shards, smallest, high):
    def one(position, shards_of):
        heights = jax.random.uniform(jax.random.fold_in(jax.random.fold_in(own_key, 6), position), (shards_of,), jnp.float32, smallest / len(shards), high / len(shards))
        return jnp.repeat(jnp.exp(heights), extent[position] // shards_of).reshape((-1,) + (1,) * (len(extent) - position - 1))

    loudness = one(*shards[0])
    for cut in shards[1:]:
        loudness = loudness * one(*cut)
    return loudness


def gaussian(key, extent, spread, reach, split=(), held_as=jnp.bfloat16):
    entries = jax.random.normal(key, extent, jnp.float32) * spread
    if len(split) > 0:
        entries = steps_of(key, extent, split, -0.22, 0.18) * entries
    return jnp.clip(entries, min=-reach, max=reach).astype(held_as)


def setup_inputs(seed: int = 0) -> dict:
    arg_keys = jax.random.split(jax.random.key(seed), 6)
    tokens = gaussian(arg_keys[0], (TOKENS, D), 1.0, 6.0, ((0, 4), (1, 8)))
    weight_in = gaussian(arg_keys[1], (D, FF), D ** -0.5, 0.0546875, ((0, 8), (1, 4)))
    weight_out = gaussian(arg_keys[2], (FF, D), FF ** -0.5, 0.0390625, ((0, 4), (1, 8)))
    bias_in = gaussian(arg_keys[3], (FF,), 0.5, 3.0, ((0, 4),))
    cotangent = gaussian(arg_keys[4], (TOKENS, D), 1.0, 6.0, ((0, 4), (1, 8)))
    return {"tokens": tokens, "weight_in": weight_in, "weight_out": weight_out, "bias_in": bias_in, "cotangent": cotangent}


gelu_coef = math.sqrt(2.0 / math.pi)
cubic_coef = 0.044715

def gelu_tanh(values):
    inner = jnp.tanh(gelu_coef * (values + cubic_coef * values * values * values))
    return 0.5 * values * (1.0 + inner)

def gelu_slope(values):
    inner = jnp.tanh(gelu_coef * (values + cubic_coef * values * values * values))
    return 0.5 * (1.0 + inner) + 0.5 * values * (1.0 - inner * inner) * gelu_coef * (1.0 + 3.0 * cubic_coef * values * values)

def rounded(values):
    return values.astype(jnp.bfloat16).astype(jnp.float32)

def reference(tokens, weight_in, weight_out, bias_in, cotangent):
    width_part = D // N_ROW
    hidden_part = FF // N_COL
    factor = 1.0 / math.sqrt(TOKENS)
    pre_gelu = jnp.zeros((TOKENS, FF), jnp.float32)
    for number in range(N_ROW):
        offset = number * width_part
        pre_gelu = pre_gelu + rounded(jnp.dot(tokens[:, offset:offset + width_part], weight_in[offset:offset + width_part, :], preferred_element_type=jnp.float32))
    pre_gelu = pre_gelu + bias_in.astype(jnp.float32)
    hidden = gelu_tanh(pre_gelu).astype(jnp.bfloat16)
    output_sum = jnp.zeros((TOKENS, D), jnp.float32)
    for number in range(N_COL):
        offset = number * hidden_part
        output_sum = output_sum + rounded(jnp.dot(hidden[:, offset:offset + hidden_part], weight_out[offset:offset + hidden_part, :], preferred_element_type=jnp.float32))
    output = output_sum.astype(jnp.bfloat16)
    back_grad = jnp.zeros((TOKENS, FF), jnp.float32)
    for number in range(N_ROW):
        offset = number * width_part
        back_grad = back_grad + rounded(jnp.dot(cotangent[:, offset:offset + width_part], weight_out[:, offset:offset + width_part].T, preferred_element_type=jnp.float32))
    slope_grad = (back_grad * gelu_slope(pre_gelu)).astype(jnp.bfloat16)
    input_sum = jnp.zeros((TOKENS, D), jnp.float32)
    for number in range(N_COL):
        offset = number * hidden_part
        input_sum = input_sum + rounded(jnp.dot(slope_grad[:, offset:offset + hidden_part], weight_in[:, offset:offset + hidden_part].T, preferred_element_type=jnp.float32))
    grad_tokens = input_sum.astype(jnp.bfloat16)
    grad_weight_in = (jnp.dot(tokens.T, slope_grad, preferred_element_type=jnp.float32) * factor).astype(jnp.bfloat16)
    grad_weight_out = (jnp.dot(hidden.T, cotangent, preferred_element_type=jnp.float32) * factor).astype(jnp.bfloat16)
    grad_bias = lax.optimization_barrier(jnp.sum(slope_grad, axis=0, dtype=jnp.float32)) * factor
    return (output, grad_tokens, grad_weight_in, grad_weight_out, grad_bias)
```

```python
import functools
import math

import jax
import jax.numpy as jnp
from jax import lax
from jax.experimental import pallas as pl
from jax.experimental.pallas import tpu as pltpu
from jax.sharding import PartitionSpec as P

gelu_coef = math.sqrt(2.0 / math.pi)
cubic_coef = 0.044715


def gelu_tanh(values):
    inner = jnp.tanh(gelu_coef * (values + cubic_coef * values * values * values))
    return 0.5 * values * (1.0 + inner)


def gelu_slope(values):
    inner = jnp.tanh(gelu_coef * (values + cubic_coef * values * values * values))
    return 0.5 * (1.0 + inner) + 0.5 * values * (1.0 - inner * inner) * gelu_coef * (
        1.0 + 3.0 * cubic_coef * values * values
    )


MESH = pl.DeviceIdType.MESH
wide = 256
row_step = 64


def over_tokens(left, right):
    return lax.dot_general(
        left, right, (((0,), (0,)), ((), ())), preferred_element_type=jnp.float32
    )


def times_transposed(left, right):
    return lax.dot_general(
        left, right, (((1,), (1,)), ((), ())), preferred_element_type=jnp.float32
    )


def times(left, right):
    return jnp.dot(left, right, preferred_element_type=jnp.float32)


def chain_kernel(
    length, parts, tok, cot, bias, win, wout, hid_o, slope_o, out_o, gt_o,
    gathered, sums, theirs, mine, near_in, near_out, far_in, far_out, acc_o, acc_g,
    sum_send, sum_recv, pair_send, pair_recv, ring_send, ring_recv, hand_send, hand_recv,
    near_sem, far_sem, store_sem,
):
    steps = 2 * parts
    count = tok.shape[0]
    depth = tok.shape[1]
    quarter = parts * wide
    place = lax.axis_index("row")
    spot = place // 2
    core = place % 2
    partner = spot * 2 + (1 - core)

    def device(other):
        return {"row": other}

    barrier = pltpu.get_barrier_semaphore()
    pl.semaphore_signal(barrier, inc=1, device_id=device(partner), device_id_type=MESH)

    @pl.when(spot > 0)
    def _():
        pl.semaphore_signal(barrier, inc=1, device_id=device(place - 2), device_id_type=MESH)

    @pl.when(spot < length - 1)
    def _():
        pl.semaphore_signal(barrier, inc=1, device_id=device(place + 2), device_id_type=MESH)

    acc_o[...] = jnp.zeros_like(acc_o)
    acc_g[...] = jnp.zeros_like(acc_g)

    pl.semaphore_wait(barrier, 1 + jnp.where(spot > 0, 1, 0) + jnp.where(spot < length - 1, 1, 0))

    def columns(q, part):
        return pl.ds(pl.multiple_of(q * quarter + part * wide, wide), wide)

    def load(q, part, from_in, in_slot, out_slot, sem):
        first = pltpu.make_async_copy(win.at[:, columns(q, part)], in_slot, sem)
        second = pltpu.make_async_copy(wout.at[columns(q, part), :], out_slot, sem)
        return first if from_in else second

    def near_quarter(item):
        way = item // 2
        own = item % 2
        return way, own, way * 2 + jnp.where(own == 1, core, 1 - core)

    def near_copy(item, step, from_in):
        way, own, q = near_quarter(item)
        return load(q, step % parts, from_in, near_in.at[item], near_out.at[item], near_sem.at[item])

    def far_copy(way, which, step, from_in):
        slot = way * 2 + which
        return load(slot, step % parts, from_in, far_in.at[slot], far_out.at[slot], far_sem.at[slot])

    def hops(way):
        return length - 1 - spot if way == 0 else spot

    def onward(way):
        return place - 2 if way == 0 else place + 2

    def backward(way):
        return place + 2 if way == 0 else place - 2

    def sum_copy(way, step):
        return pltpu.make_async_remote_copy(
            src_ref=sums.at[way, step], dst_ref=sums.at[way, step],
            send_sem=sum_send.at[way, step], recv_sem=sum_recv.at[way, step],
            device_id=device(onward(way)), device_id_type=MESH)

    def pair_copy(way, step):
        return pltpu.make_async_remote_copy(
            src_ref=mine.at[way, steps + step % 2], dst_ref=theirs.at[way, step],
            send_sem=pair_send.at[way, step % 2], recv_sem=pair_recv.at[way, step],
            device_id=device(partner), device_id_type=MESH)

    def ring_copy(way, step):
        return pltpu.make_async_remote_copy(
            src_ref=gathered.at[way * 2 + core, step], dst_ref=gathered.at[way * 2 + core, step],
            send_sem=ring_send.at[way, step], recv_sem=ring_recv.at[way, step],
            device_id=device(backward(way)), device_id_type=MESH)

    def hand_copy(way, step, q):
        return pltpu.make_async_remote_copy(
            src_ref=gathered.at[q, step], dst_ref=gathered.at[q, step],
            send_sem=hand_send.at[way, step], recv_sem=hand_recv.at[way, step],
            device_id=device(partner), device_id_type=MESH)

    def store_copy(q, step, is_hidden):
        target = hid_o if is_hidden else slope_o
        return pltpu.make_async_copy(
            gathered.at[q, step], target.at[:, columns(q, step % parts)], store_sem.at[q, step])

    def in_rows(body):
        def one(index, carry):
            body(pl.ds(pl.multiple_of(index * row_step, row_step), row_step))
            return carry

        lax.fori_loop(0, count // row_step, one, 0)

    def wide_of(ref, way, step, rows):
        return ref[way, step, rows, :].astype(jnp.float32)

    def combine(way, step, hop):
        pair_copy(way, step).wait_recv()

        @pl.when(hop == 0)
        def _():
            def body(rows):
                total = wide_of(mine, way, step, rows) + wide_of(theirs, way, step, rows)
                sums[way, step, rows, :] = total.astype(jnp.bfloat16)

            in_rows(body)

        @pl.when(hop > 0)
        def _():
            sum_copy(way, step).wait_recv()

        def total_of(at, rows):
            return (
                wide_of(mine, way, at, rows) + wide_of(theirs, way, at, rows)
            ) + wide_of(sums, way, at, rows)

        @pl.when(jnp.logical_and(hop > 0, hop < length - 1))
        def _():
            def body(rows):
                sums[way, step, rows, :] = total_of(step, rows).astype(jnp.bfloat16)

            in_rows(body)

        @pl.when(hop < length - 1)
        def _():
            sum_copy(way, step).start()

        @pl.when(hop == length - 1)
        def _():
            q = way * 2 + core
            shift = bias[q * parts + step % parts]

            @pl.when(step < parts)
            def _():
                def body(rows):
                    pre = total_of(step, rows) + shift
                    gathered[q, step, rows, :] = gelu_tanh(pre).astype(jnp.bfloat16)

                in_rows(body)

            @pl.when(step >= parts)
            def _():
                def body(rows):
                    pre = total_of(step - parts, rows) + shift
                    slope = total_of(step, rows) * gelu_slope(pre)
                    gathered[q, step, rows, :] = slope.astype(jnp.bfloat16)

                in_rows(body)

            ring_copy(way, step).start()
            hand_copy(way, step, q).start()

    def pass_on(way, step, hop):
        ring_copy(way, step).wait_recv()

        @pl.when(hop > 0)
        def _():
            ring_copy(way, step).start()

        hand_copy(way, step, way * 2 + core).start()

    def within(step):
        return jnp.logical_and(step >= 0, step < steps)

    def both_kinds(step, act):
        @pl.when(step < parts)
        def _():
            act(True)

        @pl.when(step >= parts)
        def _():
            act(False)

    def turn(now, carry):
        @pl.when(now < steps)
        def _():
            def start(item, inner):
                both_kinds(now, lambda first: near_copy(item, now, first).start())
                return inner

            lax.fori_loop(0, 4, start, 0)

        for way in range(2):
            used = now - 2 - 2 * (length - 1) + hops(way)

            @pl.when(within(used))
            def _(way=way, used=used):
                for which in range(2):
                    both_kinds(used, lambda first: far_copy(way, which, used, not first).start())

        for way in range(2):
            hop = hops(way)
            ready = now - 1 - hop

            @pl.when(within(ready))
            def _(way=way, ready=ready, hop=hop):
                combine(way, ready, hop)

            here = now - 1 - 2 * (length - 1) + hop

            @pl.when(jnp.logical_and(within(here), hop < length - 1))
            def _(way=way, here=here, hop=hop):
                pass_on(way, here, hop)

        @pl.when(now < steps)
        def _():
            def one(item, inner):
                way, own, _ = near_quarter(item)
                slot = jnp.where(own == 1, now, steps + now % 2)

                @pl.when(jnp.logical_and(own == 0, now >= 2))
                def _():
                    pair_copy(way, now).wait_send()

                @pl.when(now < parts)
                def _():
                    near_copy(item, now, True).wait()
                    mine[way, slot] = times(tok[...], near_in[item]).astype(jnp.bfloat16)

                @pl.when(now >= parts)
                def _():
                    near_copy(item, now, False).wait()
                    mine[way, slot] = times_transposed(cot[...], near_out[item]).astype(jnp.bfloat16)

                @pl.when(own == 0)
                def _():
                    pair_copy(way, now).start()

                return inner

            lax.fori_loop(0, 4, one, 0)

        def use(way, inner):
            hop = jnp.where(way == 0, hops(0), hops(1))
            used = now - 2 - 2 * (length - 1) + hop

            @pl.when(within(used))
            def _():
                hand_copy(way, used, way * 2 + 1 - core).wait_recv()
                for which in range(2):
                    both_kinds(used, lambda first: store_copy(way * 2 + which, used, first).start())
                slab = depth // 3

                @pl.when(used < parts)
                def _():
                    for which in range(2):
                        far_copy(way, which, used, False).wait()
                    for third in range(3):
                        at = slice(third * slab, (third + 1) * slab)
                        acc_o[:, at] += times(gathered[way * 2, used], far_out[way * 2, :, at]) + times(
                            gathered[way * 2 + 1, used], far_out[way * 2 + 1, :, at])

                @pl.when(used >= parts)
                def _():
                    for which in range(2):
                        far_copy(way, which, used, True).wait()
                    for third in range(3):
                        at = slice(third * slab, (third + 1) * slab)
                        acc_g[:, at] += times_transposed(
                            gathered[way * 2, used], far_in[way * 2, at, :]
                        ) + times_transposed(gathered[way * 2 + 1, used], far_in[way * 2 + 1, at, :])

            return inner

        lax.fori_loop(0, 2, use, 0)
        return carry

    lax.fori_loop(0, steps + 2 * length, turn, 0)
    out_o[...] = acc_o[...].astype(jnp.bfloat16)
    gt_o[...] = acc_g[...].astype(jnp.bfloat16)

    def finish(step, carry):
        for way in range(2):
            hop = hops(way)

            @pl.when(hop < length - 1)
            def _(way=way):
                sum_copy(way, step).wait_send()

            @pl.when(hop > 0)
            def _(way=way):
                ring_copy(way, step).wait_send()

            hand_copy(way, step, way * 2 + core).wait_send()
            for which in range(2):
                both_kinds(step, lambda first: store_copy(way * 2 + which, step, first).wait())
        return carry

    lax.fori_loop(0, steps, finish, 0)
    for way in range(2):
        for step in (steps - 2, steps - 1):
            pair_copy(way, step).wait_send()


def chain(length, tokens_all, cotangent_all, bias_wide, weight_in, weight_out):
    count, depth = tokens_all.shape
    hidden_units = weight_in.shape[1]
    parts = hidden_units // (4 * wide)
    steps = 2 * parts
    bf16 = jnp.bfloat16
    vmem = pl.BlockSpec(memory_space=pltpu.VMEM)
    anywhere = pl.BlockSpec(memory_space=pl.ANY)
    dma = pltpu.SemaphoreType.DMA
    return pl.pallas_call(
        functools.partial(chain_kernel, length, parts),
        out_shape=(
            jax.ShapeDtypeStruct((count, hidden_units), bf16),
            jax.ShapeDtypeStruct((count, hidden_units), bf16),
            jax.ShapeDtypeStruct((count, depth), bf16),
            jax.ShapeDtypeStruct((count, depth), bf16),
        ),
        in_specs=[vmem, vmem, vmem, anywhere, anywhere],
        out_specs=(anywhere, anywhere, vmem, vmem),
        scratch_shapes=[
            pltpu.VMEM((4, steps, count, wide), bf16),
            pltpu.VMEM((2, steps, count, wide), bf16),
            pltpu.VMEM((2, steps, count, wide), bf16),
            pltpu.VMEM((2, steps + 2, count, wide), bf16),
            pltpu.VMEM((4, depth, wide), bf16),
            pltpu.VMEM((4, wide, depth), bf16),
            pltpu.VMEM((4, depth, wide), bf16),
            pltpu.VMEM((4, wide, depth), bf16),
            pltpu.VMEM((count, depth), jnp.float32),
            pltpu.VMEM((count, depth), jnp.float32),
            dma((2, steps)), dma((2, steps)), dma((2, 2)), dma((2, steps)),
            dma((2, steps)), dma((2, steps)), dma((2, steps)), dma((2, steps)),
            dma((4,)), dma((4,)), dma((4, steps)),
        ],
        compiler_params=pltpu.CompilerParams(
            collective_id=0, has_side_effects=True, vmem_limit_bytes=60 * 1024 * 1024
        ),
    )(tokens_all, cotangent_all, bias_wide.reshape(-1, 1, wide), weight_in, weight_out)


def slope_kernel(factor, left, right, grad, total, turned):
    @pl.when(pl.program_id(0) == 0)
    def _():
        turned[...] = left[...].T

    grad[...] = (times(turned[...], right[...]) * factor).astype(jnp.bfloat16)
    total[...] = jnp.sum(right[...].astype(jnp.float32), axis=0, keepdims=True) * factor


def slope_grads(factor, left, right):
    count, depth = left.shape
    units = right.shape[1]
    block = 2 * wide
    return pl.pallas_call(
        functools.partial(slope_kernel, factor),
        grid=(units // block,),
        out_shape=(
            jax.ShapeDtypeStruct((depth, units), jnp.bfloat16),
            jax.ShapeDtypeStruct((1, units), jnp.float32),
        ),
        in_specs=[
            pl.BlockSpec((count, depth), lambda j: (0, 0)),
            pl.BlockSpec((count, block), lambda j: (0, j)),
        ],
        out_specs=(
            pl.BlockSpec((depth, block), lambda j: (0, j)),
            pl.BlockSpec((1, block), lambda j: (0, j)),
        ),
        scratch_shapes=[pltpu.VMEM((depth, count), jnp.bfloat16)],
        compiler_params=pltpu.CompilerParams(vmem_limit_bytes=40 * 1024 * 1024),
        cost_estimate=pl.CostEstimate(
            flops=2 * count * depth * units,
            bytes_accessed=2 * (count * depth + count * units + depth * units),
            transcendentals=0,
        ),
    )(left, right)


def per_device(length, tokens, weight_in, weight_out, bias_in, cotangent):
    rows_here = tokens.shape[0]
    total_rows = rows_here * lax.axis_size("col")
    factor = 1.0 / math.sqrt(total_rows)
    tokens_all = lax.all_gather(tokens, "col", axis=0, tiled=True)
    cotangent_all = lax.all_gather(cotangent, "col", axis=0, tiled=True)
    hidden_all, slope_all, output, grad_tokens = chain(
        length, tokens_all, cotangent_all, bias_in.astype(jnp.float32), weight_in, weight_out
    )
    output = lax.psum_scatter(output, "col", scatter_dimension=0, tiled=True)
    grad_tokens = lax.psum_scatter(grad_tokens, "col", scatter_dimension=0, tiled=True)
    grad_weight_out = (over_tokens(hidden_all, cotangent_all) * factor).astype(jnp.bfloat16)
    grad_weight_in, grad_bias = slope_grads(factor, tokens_all, slope_all)
    grad_bias = grad_bias.reshape(-1)
    return (output, grad_tokens, grad_weight_in, grad_weight_out, grad_bias)


def solution(mesh):
    placed = (P("col", "row"), P("row", "col"), P("col", "row"), P("col"), P("col", "row"))
    return jax.shard_map(
        functools.partial(per_device, mesh.shape["row"] // 2),
        mesh=mesh,
        in_specs=placed,
        out_specs=(P("col", "row"), P("col", "row"), P("row", "col"), P("col", "row"), P("col")),
        check_vma=False,
    )
```

```python
import functools
import math

import jax
import jax.numpy as jnp
from jax import lax
from jax.experimental import pallas as pl
from jax.experimental.pallas import tpu as pltpu
from jax.sharding import PartitionSpec as P

gelu_coef = math.sqrt(2.0 / math.pi)
cubic_coef = 0.044715


def gelu_tanh(values):
    inner = jnp.tanh(gelu_coef * (values + cubic_coef * values * values * values))
    return 0.5 * values * (1.0 + inner)


def gelu_slope(values):
    inner = jnp.tanh(gelu_coef * (values + cubic_coef * values * values * values))
    return 0.5 * (1.0 + inner) + 0.5 * values * (1.0 - inner * inner) * gelu_coef * (
        1.0 + 3.0 * cubic_coef * values * values
    )


MESH = pl.DeviceIdType.MESH
wide = 256
row_step = 64


def over_tokens(left, right):
    return lax.dot_general(
        left, right, (((0,), (0,)), ((), ())), preferred_element_type=jnp.float32
    )


def times_transposed(left, right):
    return lax.dot_general(
        left, right, (((1,), (1,)), ((), ())), preferred_element_type=jnp.float32
    )


def times(left, right):
    return jnp.dot(left, right, preferred_element_type=jnp.float32)


def chain_kernel(
    length, groups, parts, tok_here, cot_here, bias, win, wout, hid_o, slope_o, out_o, gt_o, tok_o, cot_o,
    tok, cot, staged, landed, gathered, sums, theirs, mine, near_in, near_out, far_in, far_out, acc_o, acc_g,
    sum_send, sum_recv, pair_send, pair_recv, ring_send, ring_recv, hand_send, hand_recv,
    near_sem, far_sem, store_sem, own_sem, whole_sem, share_send, share_recv, out_send, out_recv,
):
    steps = 2 * parts
    count = tok.shape[0]
    depth = tok.shape[1]
    quarter = parts * wide
    place = lax.axis_index("row")
    spot = place // 2
    core = place % 2
    partner = spot * 2 + (1 - core)
    group = lax.axis_index("col")
    rows_each = count // groups

    def peer(offset):
        return lax.rem(group + offset + groups, groups)

    def rows_of(which):
        return pl.ds(pl.multiple_of(which * rows_each, rows_each), rows_each)

    def own_copy(kind):
        source, target = ((tok_here, tok), (cot_here, cot))[kind]
        return pltpu.make_async_copy(source, target.at[rows_of(group), :], own_sem.at[kind])

    def whole_copy(kind):
        source, target = ((tok, tok_o), (cot, cot_o))[kind]
        return pltpu.make_async_copy(source, target, whole_sem.at[kind])

    def share_copy(kind, offset, rows):
        ref = (tok, cot)[kind]
        return pltpu.make_async_remote_copy(
            src_ref=ref.at[rows_of(rows), :], dst_ref=ref.at[rows_of(rows), :],
            send_sem=share_send.at[kind, offset], recv_sem=share_recv.at[kind, offset],
            device_id={"col": peer(offset)}, device_id_type=MESH)

    def share(kind):
        for offset in range(1, groups):
            share_copy(kind, offset, group).start()

    def shared(kind):
        for offset in range(1, groups):
            share_copy(kind, offset, peer(-offset)).wait_recv()
        whole_copy(kind).start()

    def out_copy(offset):
        return pltpu.make_async_remote_copy(
            src_ref=staged.at[rows_of(peer(offset)), :], dst_ref=landed.at[offset - 1],
            send_sem=out_send.at[offset], recv_sem=out_recv.at[offset],
            device_id={"col": peer(offset)}, device_id_type=MESH)

    own_copy(0).start()
    own_copy(1).start()

    def device(other):
        return {"row": other}

    barrier = pltpu.get_barrier_semaphore()
    pl.semaphore_signal(barrier, inc=1, device_id=device(partner), device_id_type=MESH)
    for offset in range(1, groups):
        pl.semaphore_signal(barrier, inc=1, device_id={"col": peer(offset)}, device_id_type=MESH)

    @pl.when(spot > 0)
    def _():
        pl.semaphore_signal(barrier, inc=1, device_id=device(place - 2), device_id_type=MESH)

    @pl.when(spot < length - 1)
    def _():
        pl.semaphore_signal(barrier, inc=1, device_id=device(place + 2), device_id_type=MESH)

    own_copy(0).wait()
    own_copy(1).wait()
    pl.semaphore_wait(barrier, groups + jnp.where(spot > 0, 1, 0) + jnp.where(spot < length - 1, 1, 0))

    share(0)
    acc_o[...] = jnp.zeros_like(acc_o)
    acc_g[...] = jnp.zeros_like(acc_g)
    shared(0)
    share(1)

    def columns(q, part):
        return pl.ds(pl.multiple_of(q * quarter + part * wide, wide), wide)

    def load(q, part, from_in, in_slot, out_slot, sem):
        first = pltpu.make_async_copy(win.at[:, columns(q, part)], in_slot, sem)
        second = pltpu.make_async_copy(wout.at[columns(q, part), :], out_slot, sem)
        return first if from_in else second

    def near_quarter(item):
        way = item // 2
        own = item % 2
        return way, own, way * 2 + jnp.where(own == 1, core, 1 - core)

    def near_copy(item, step, from_in):
        way, own, q = near_quarter(item)
        return load(q, step % parts, from_in, near_in.at[item], near_out.at[item], near_sem.at[item])

    def far_copy(way, which, step, from_in):
        slot = way * 2 + which
        return load(slot, step % parts, from_in, far_in.at[slot], far_out.at[slot], far_sem.at[slot])

    def hops(way):
        return length - 1 - spot if way == 0 else spot

    def onward(way):
        return place - 2 if way == 0 else place + 2

    def backward(way):
        return place + 2 if way == 0 else place - 2

    def sum_copy(way, step):
        return pltpu.make_async_remote_copy(
            src_ref=sums.at[way, step], dst_ref=sums.at[way, step],
            send_sem=sum_send.at[way, step], recv_sem=sum_recv.at[way, step],
            device_id=device(onward(way)), device_id_type=MESH)

    def pair_copy(way, step):
        return pltpu.make_async_remote_copy(
            src_ref=mine.at[way, steps + step % 2], dst_ref=theirs.at[way, step],
            send_sem=pair_send.at[way, step % 2], recv_sem=pair_recv.at[way, step],
            device_id=device(partner), device_id_type=MESH)

    def ring_copy(way, step):
        return pltpu.make_async_remote_copy(
            src_ref=gathered.at[way * 2 + core, step], dst_ref=gathered.at[way * 2 + core, step],
            send_sem=ring_send.at[way, step], recv_sem=ring_recv.at[way, step],
            device_id=device(backward(way)), device_id_type=MESH)

    def hand_copy(way, step, q):
        return pltpu.make_async_remote_copy(
            src_ref=gathered.at[q, step], dst_ref=gathered.at[q, step],
            send_sem=hand_send.at[way, step], recv_sem=hand_recv.at[way, step],
            device_id=device(partner), device_id_type=MESH)

    def store_copy(q, step, is_hidden):
        target = hid_o if is_hidden else slope_o
        return pltpu.make_async_copy(
            gathered.at[q, step], target.at[:, columns(q, step % parts)], store_sem.at[q, step])

    def in_rows(body):
        def one(index, carry):
            body(pl.ds(pl.multiple_of(index * row_step, row_step), row_step))
            return carry

        lax.fori_loop(0, count // row_step, one, 0)

    def wide_of(ref, way, step, rows):
        return ref[way, step, rows, :].astype(jnp.float32)

    def combine(way, step, hop):
        pair_copy(way, step).wait_recv()

        @pl.when(hop == 0)
        def _():
            def body(rows):
                total = wide_of(mine, way, step, rows) + wide_of(theirs, way, step, rows)
                sums[way, step, rows, :] = total.astype(jnp.bfloat16)

            in_rows(body)

        @pl.when(hop > 0)
        def _():
            sum_copy(way, step).wait_recv()

        def total_of(at, rows):
            return (
                wide_of(mine, way, at, rows) + wide_of(theirs, way, at, rows)
            ) + wide_of(sums, way, at, rows)

        @pl.when(jnp.logical_and(hop > 0, hop < length - 1))
        def _():
            def body(rows):
                sums[way, step, rows, :] = total_of(step, rows).astype(jnp.bfloat16)

            in_rows(body)

        @pl.when(hop < length - 1)
        def _():
            sum_copy(way, step).start()

        @pl.when(hop == length - 1)
        def _():
            q = way * 2 + core
            shift = bias[q * parts + step % parts]

            @pl.when(step < parts)
            def _():
                def body(rows):
                    pre = total_of(step, rows) + shift
                    gathered[q, step, rows, :] = gelu_tanh(pre).astype(jnp.bfloat16)

                in_rows(body)

            @pl.when(step >= parts)
            def _():
                def body(rows):
                    pre = total_of(step - parts, rows) + shift
                    slope = total_of(step, rows) * gelu_slope(pre)
                    gathered[q, step, rows, :] = slope.astype(jnp.bfloat16)

                in_rows(body)

            ring_copy(way, step).start()
            hand_copy(way, step, q).start()

    def pass_on(way, step, hop):
        ring_copy(way, step).wait_recv()

        @pl.when(hop > 0)
        def _():
            ring_copy(way, step).start()

        hand_copy(way, step, way * 2 + core).start()

    def within(step):
        return jnp.logical_and(step >= 0, step < steps)

    def both_kinds(step, act):
        @pl.when(step < parts)
        def _():
            act(True)

        @pl.when(step >= parts)
        def _():
            act(False)

    def turn(now, carry):
        @pl.when(now < steps)
        def _():
            def start(item, inner):
                both_kinds(now, lambda first: near_copy(item, now, first).start())
                return inner

            lax.fori_loop(0, 4, start, 0)

        for way in range(2):
            used = now - 2 - 2 * (length - 1) + hops(way)

            @pl.when(within(used))
            def _(way=way, used=used):
                for which in range(2):
                    both_kinds(used, lambda first: far_copy(way, which, used, not first).start())

        for way in range(2):
            hop = hops(way)
            ready = now - 1 - hop

            @pl.when(within(ready))
            def _(way=way, ready=ready, hop=hop):
                combine(way, ready, hop)

        @pl.when(now == parts)
        def _():
            shared(1)

        @pl.when(now < steps)
        def _():
            def one(item, inner):
                way, own, _ = near_quarter(item)
                slot = jnp.where(own == 1, now, steps + now % 2)

                @pl.when(jnp.logical_and(own == 0, now >= 2))
                def _():
                    pair_copy(way, now).wait_send()

                @pl.when(now < parts)
                def _():
                    near_copy(item, now, True).wait()
                    mine[way, slot] = times(tok[...], near_in[item]).astype(jnp.bfloat16)

                @pl.when(now >= parts)
                def _():
                    near_copy(item, now, False).wait()
                    mine[way, slot] = times_transposed(cot[...], near_out[item]).astype(jnp.bfloat16)

                @pl.when(own == 0)
                def _():
                    pair_copy(way, now).start()

                return inner

            lax.fori_loop(0, 4, one, 0)

        for way in range(2):
            hop = hops(way)
            here = now - 1 - 2 * (length - 1) + hop

            @pl.when(jnp.logical_and(within(here), hop < length - 1))
            def _(way=way, here=here, hop=hop):
                pass_on(way, here, hop)

        def use(way, inner):
            hop = jnp.where(way == 0, hops(0), hops(1))
            used = now - 2 - 2 * (length - 1) + hop

            @pl.when(within(used))
            def _():
                hand_copy(way, used, way * 2 + 1 - core).wait_recv()
                for which in range(2):
                    both_kinds(used, lambda first: store_copy(way * 2 + which, used, first).start())
                slab = depth // 3

                @pl.when(used < parts)
                def _():
                    for which in range(2):
                        far_copy(way, which, used, False).wait()
                    for third in range(3):
                        at = slice(third * slab, (third + 1) * slab)
                        acc_o[:, at] += times(gathered[way * 2, used], far_out[way * 2, :, at]) + times(
                            gathered[way * 2 + 1, used], far_out[way * 2 + 1, :, at])

                @pl.when(used >= parts)
                def _():
                    for which in range(2):
                        far_copy(way, which, used, True).wait()
                    for third in range(3):
                        at = slice(third * slab, (third + 1) * slab)
                        acc_g[:, at] += times_transposed(
                            gathered[way * 2, used], far_in[way * 2, at, :]
                        ) + times_transposed(gathered[way * 2 + 1, used], far_in[way * 2 + 1, at, :])

            return inner

        lax.fori_loop(0, 2, use, 0)

        @pl.when(now == parts - 1 + 2 * length)
        def _():
            staged[...] = acc_o[...].astype(jnp.bfloat16)
            for offset in range(1, groups):
                out_copy(offset).start()

        return carry

    lax.fori_loop(0, steps + 2 * length, turn, 0)
    for offset in range(1, groups):
        out_copy(offset).wait_recv()
    total = acc_o[rows_of(group), :]
    for offset in range(1, groups):
        total = total + landed[offset - 1].astype(jnp.float32)
    out_o[...] = total.astype(jnp.bfloat16)
    gt_o[...] = acc_g[...].astype(jnp.bfloat16)

    def finish(step, carry):
        for way in range(2):
            hop = hops(way)

            @pl.when(hop < length - 1)
            def _(way=way):
                sum_copy(way, step).wait_send()

            @pl.when(hop > 0)
            def _(way=way):
                ring_copy(way, step).wait_send()

            hand_copy(way, step, way * 2 + core).wait_send()
            for which in range(2):
                both_kinds(step, lambda first: store_copy(way * 2 + which, step, first).wait())
        return carry

    lax.fori_loop(0, steps, finish, 0)
    for kind in range(2):
        whole_copy(kind).wait()
        for offset in range(1, groups):
            share_copy(kind, offset, group).wait_send()
    for offset in range(1, groups):
        out_copy(offset).wait_send()
    for way in range(2):
        for step in (steps - 2, steps - 1):
            pair_copy(way, step).wait_send()


def chain(length, groups, tokens, cotangent, bias_wide, weight_in, weight_out):
    rows_each, depth = tokens.shape
    count = rows_each * groups
    hidden_units = weight_in.shape[1]
    parts = hidden_units // (4 * wide)
    steps = 2 * parts
    bf16 = jnp.bfloat16
    vmem = pl.BlockSpec(memory_space=pltpu.VMEM)
    anywhere = pl.BlockSpec(memory_space=pl.ANY)
    dma = pltpu.SemaphoreType.DMA
    return pl.pallas_call(
        functools.partial(chain_kernel, length, groups, parts),
        out_shape=(
            jax.ShapeDtypeStruct((count, hidden_units), bf16),
            jax.ShapeDtypeStruct((count, hidden_units), bf16),
            jax.ShapeDtypeStruct((rows_each, depth), bf16),
            jax.ShapeDtypeStruct((count, depth), bf16),
            jax.ShapeDtypeStruct((count, depth), bf16),
            jax.ShapeDtypeStruct((count, depth), bf16),
        ),
        in_specs=[anywhere, anywhere, vmem, anywhere, anywhere],
        out_specs=(anywhere, anywhere, vmem, vmem, anywhere, anywhere),
        scratch_shapes=[
            pltpu.VMEM((count, depth), bf16),
            pltpu.VMEM((count, depth), bf16),
            pltpu.VMEM((count, depth), bf16),
            pltpu.VMEM((groups - 1, rows_each, depth), bf16),
            pltpu.VMEM((4, steps, count, wide), bf16),
            pltpu.VMEM((2, steps, count, wide), bf16),
            pltpu.VMEM((2, steps, count, wide), bf16),
            pltpu.VMEM((2, steps + 2, count, wide), bf16),
            pltpu.VMEM((4, depth, wide), bf16),
            pltpu.VMEM((4, wide, depth), bf16),
            pltpu.VMEM((4, depth, wide), bf16),
            pltpu.VMEM((4, wide, depth), bf16),
            pltpu.VMEM((count, depth), jnp.float32),
            pltpu.VMEM((count, depth), jnp.float32),
            dma((2, steps)), dma((2, steps)), dma((2, 2)), dma((2, steps)),
            dma((2, steps)), dma((2, steps)), dma((2, steps)), dma((2, steps)),
            dma((4,)), dma((4,)), dma((4, steps)),
            dma((2,)), dma((2,)), dma((2, groups)), dma((2, groups)), dma((groups,)), dma((groups,)),
        ],
        compiler_params=pltpu.CompilerParams(
            collective_id=0, has_side_effects=True, vmem_limit_bytes=61 * 1024 * 1024
        ),
    )(tokens, cotangent, bias_wide.reshape(-1, 1, wide), weight_in, weight_out)


def slope_kernel(factor, left, right, grad, total, turned):
    @pl.when(pl.program_id(0) == 0)
    def _():
        turned[...] = left[...].T

    grad[...] = (times(turned[...], right[...]) * factor).astype(jnp.bfloat16)
    total[...] = jnp.sum(right[...].astype(jnp.float32), axis=0, keepdims=True) * factor


def slope_grads(factor, left, right):
    count, depth = left.shape
    units = right.shape[1]
    block = 2 * wide
    return pl.pallas_call(
        functools.partial(slope_kernel, factor),
        grid=(units // block,),
        out_shape=(
            jax.ShapeDtypeStruct((depth, units), jnp.bfloat16),
            jax.ShapeDtypeStruct((1, units), jnp.float32),
        ),
        in_specs=[
            pl.BlockSpec((count, depth), lambda j: (0, 0)),
            pl.BlockSpec((count, block), lambda j: (0, j)),
        ],
        out_specs=(
            pl.BlockSpec((depth, block), lambda j: (0, j)),
            pl.BlockSpec((1, block), lambda j: (0, j)),
        ),
        scratch_shapes=[pltpu.VMEM((depth, count), jnp.bfloat16)],
        compiler_params=pltpu.CompilerParams(vmem_limit_bytes=40 * 1024 * 1024),
        cost_estimate=pl.CostEstimate(
            flops=2 * count * depth * units,
            bytes_accessed=2 * (count * depth + count * units + depth * units),
            transcendentals=0,
        ),
    )(left, right)


def per_device(length, groups, tokens, weight_in, weight_out, bias_in, cotangent):
    rows_here = tokens.shape[0]
    total_rows = rows_here * lax.axis_size("col")
    factor = 1.0 / math.sqrt(total_rows)
    hidden_all, slope_all, output, grad_tokens, tokens_all, cotangent_all = chain(
        length, groups, tokens, cotangent, bias_in.astype(jnp.float32), weight_in, weight_out
    )
    grad_tokens = lax.psum_scatter(grad_tokens, "col", scatter_dimension=0, tiled=True)
    grad_weight_out = (over_tokens(hidden_all, cotangent_all) * factor).astype(jnp.bfloat16)
    grad_weight_in, grad_bias = slope_grads(factor, tokens_all, slope_all)
    grad_bias = grad_bias.reshape(-1)
    return (output, grad_tokens, grad_weight_in, grad_weight_out, grad_bias)


def solution(mesh):
    placed = (P("col", "row"), P("row", "col"), P("col", "row"), P("col"), P("col", "row"))
    return jax.shard_map(
        functools.partial(per_device, mesh.shape["row"] // 2, mesh.shape["col"]),
        mesh=mesh,
        in_specs=placed,
        out_specs=(P("col", "row"), P("col", "row"), P("row", "col"), P("col", "row"), P("col")),
        check_vma=False,
    )
```

```python
import functools
import math

import jax
import jax.numpy as jnp
from jax import lax
from jax.experimental import pallas as pl
from jax.experimental.pallas import tpu as pltpu
from jax.sharding import PartitionSpec as P

gelu_coef = math.sqrt(2.0 / math.pi)
cubic_coef = 0.044715


def gelu_tanh(values):
    inner = jnp.tanh(gelu_coef * (values + cubic_coef * values * values * values))
    return 0.5 * values * (1.0 + inner)


def gelu_slope(values):
    inner = jnp.tanh(gelu_coef * (values + cubic_coef * values * values * values))
    return 0.5 * (1.0 + inner) + 0.5 * values * (1.0 - inner * inner) * gelu_coef * (
        1.0 + 3.0 * cubic_coef * values * values
    )


MESH = pl.DeviceIdType.MESH
wide = 256
row_step = 64


def times_transposed(left, right):
    return lax.dot_general(
        left, right, (((1,), (1,)), ((), ())), preferred_element_type=jnp.float32
    )


def times(left, right):
    return jnp.dot(left, right, preferred_element_type=jnp.float32)


def chain_kernel(
    length, groups, parts, tok_here, cot_here, bias, win, wout, hid_o, slope_o, out_o, gt_o, tok_o, cot_o,
    tok, cot, staged, landed, gathered, sums, theirs, mine, near_in, near_out, far_in, far_out, acc_o, acc_g,
    sum_send, sum_recv, pair_send, pair_recv, ring_send, ring_recv, hand_send, hand_recv,
    near_sem, far_sem, store_sem, own_sem, whole_sem, share_send, share_recv, out_send, out_recv,
):
    steps = 2 * parts
    count = tok.shape[0]
    depth = tok.shape[1]
    quarter = parts * wide
    place = lax.axis_index("row")
    spot = place // 2
    core = place % 2
    partner = spot * 2 + (1 - core)
    group = lax.axis_index("col")
    rows_each = count // groups

    def peer(offset):
        return lax.rem(group + offset + groups, groups)

    def rows_of(which):
        return pl.ds(pl.multiple_of(which * rows_each, rows_each), rows_each)

    def own_copy(kind):
        source, target = ((tok_here, tok), (cot_here, cot))[kind]
        return pltpu.make_async_copy(source, target.at[rows_of(group), :], own_sem.at[kind])

    def whole_copy(kind):
        source, target = ((tok, tok_o), (cot, cot_o))[kind]
        return pltpu.make_async_copy(source, target, whole_sem.at[kind])

    def share_copy(kind, offset, rows):
        ref = (tok, cot)[kind]
        return pltpu.make_async_remote_copy(
            src_ref=ref.at[rows_of(rows), :], dst_ref=ref.at[rows_of(rows), :],
            send_sem=share_send.at[kind, offset], recv_sem=share_recv.at[kind, offset],
            device_id={"col": peer(offset)}, device_id_type=MESH)

    def share(kind):
        for offset in range(1, groups):
            share_copy(kind, offset, group).start()

    def shared(kind):
        for offset in range(1, groups):
            share_copy(kind, offset, peer(-offset)).wait_recv()
        whole_copy(kind).start()

    def out_copy(offset):
        return pltpu.make_async_remote_copy(
            src_ref=staged.at[rows_of(peer(offset)), :], dst_ref=landed.at[offset - 1],
            send_sem=out_send.at[offset], recv_sem=out_recv.at[offset],
            device_id={"col": peer(offset)}, device_id_type=MESH)

    own_copy(0).start()
    own_copy(1).start()

    def device(other):
        return {"row": other}

    barrier = pltpu.get_barrier_semaphore()
    pl.semaphore_signal(barrier, inc=1, device_id=device(partner), device_id_type=MESH)
    for offset in range(1, groups):
        pl.semaphore_signal(barrier, inc=1, device_id={"col": peer(offset)}, device_id_type=MESH)

    @pl.when(spot > 0)
    def _():
        pl.semaphore_signal(barrier, inc=1, device_id=device(place - 2), device_id_type=MESH)

    @pl.when(spot < length - 1)
    def _():
        pl.semaphore_signal(barrier, inc=1, device_id=device(place + 2), device_id_type=MESH)

    own_copy(0).wait()
    own_copy(1).wait()
    pl.semaphore_wait(barrier, groups + jnp.where(spot > 0, 1, 0) + jnp.where(spot < length - 1, 1, 0))

    share(0)
    acc_o[...] = jnp.zeros_like(acc_o)
    acc_g[...] = jnp.zeros_like(acc_g)
    shared(0)
    share(1)

    def columns(q, part):
        return pl.ds(pl.multiple_of(q * quarter + part * wide, wide), wide)

    def load(q, part, from_in, in_slot, out_slot, sem):
        first = pltpu.make_async_copy(win.at[:, columns(q, part)], in_slot, sem)
        second = pltpu.make_async_copy(wout.at[columns(q, part), :], out_slot, sem)
        return first if from_in else second

    def near_quarter(item):
        way = item // 2
        own = item % 2
        return way, own, way * 2 + jnp.where(own == 1, core, 1 - core)

    def near_copy(item, step, from_in):
        way, own, q = near_quarter(item)
        return load(q, step % parts, from_in, near_in.at[item], near_out.at[item], near_sem.at[item])

    def far_copy(way, which, step, from_in):
        slot = way * 2 + which
        return load(slot, step % parts, from_in, far_in.at[slot], far_out.at[slot], far_sem.at[slot])

    def hops(way):
        return length - 1 - spot if way == 0 else spot

    def onward(way):
        return place - 2 if way == 0 else place + 2

    def backward(way):
        return place + 2 if way == 0 else place - 2

    def sum_copy(way, step):
        return pltpu.make_async_remote_copy(
            src_ref=sums.at[way, step], dst_ref=sums.at[way, step],
            send_sem=sum_send.at[way, step], recv_sem=sum_recv.at[way, step],
            device_id=device(onward(way)), device_id_type=MESH)

    def pair_copy(way, step):
        return pltpu.make_async_remote_copy(
            src_ref=mine.at[way, steps + step % 2], dst_ref=theirs.at[way, step],
            send_sem=pair_send.at[way, step % 2], recv_sem=pair_recv.at[way, step],
            device_id=device(partner), device_id_type=MESH)

    def ring_copy(way, step):
        return pltpu.make_async_remote_copy(
            src_ref=gathered.at[way * 2 + core, step], dst_ref=gathered.at[way * 2 + core, step],
            send_sem=ring_send.at[way, step], recv_sem=ring_recv.at[way, step],
            device_id=device(backward(way)), device_id_type=MESH)

    def hand_copy(way, step, q):
        return pltpu.make_async_remote_copy(
            src_ref=gathered.at[q, step], dst_ref=gathered.at[q, step],
            send_sem=hand_send.at[way, step], recv_sem=hand_recv.at[way, step],
            device_id=device(partner), device_id_type=MESH)

    def store_copy(q, step, is_hidden):
        target = hid_o if is_hidden else slope_o
        return pltpu.make_async_copy(
            gathered.at[q, step], target.at[:, columns(q, step % parts)], store_sem.at[q, step])

    def in_rows(body):
        def one(index, carry):
            body(pl.ds(pl.multiple_of(index * row_step, row_step), row_step))
            return carry

        lax.fori_loop(0, count // row_step, one, 0)

    def wide_of(ref, way, step, rows):
        return ref[way, step, rows, :].astype(jnp.float32)

    def combine(way, step, hop):
        pair_copy(way, step).wait_recv()

        @pl.when(hop == 0)
        def _():
            def body(rows):
                total = wide_of(mine, way, step, rows) + wide_of(theirs, way, step, rows)
                sums[way, step, rows, :] = total.astype(jnp.bfloat16)

            in_rows(body)

        @pl.when(hop > 0)
        def _():
            sum_copy(way, step).wait_recv()

        def total_of(at, rows):
            return (
                wide_of(mine, way, at, rows) + wide_of(theirs, way, at, rows)
            ) + wide_of(sums, way, at, rows)

        @pl.when(jnp.logical_and(hop > 0, hop < length - 1))
        def _():
            def body(rows):
                sums[way, step, rows, :] = total_of(step, rows).astype(jnp.bfloat16)

            in_rows(body)

        @pl.when(hop < length - 1)
        def _():
            sum_copy(way, step).start()

        @pl.when(hop == length - 1)
        def _():
            q = way * 2 + core
            shift = bias[q * parts + step % parts]

            @pl.when(step < parts)
            def _():
                def body(rows):
                    pre = total_of(step, rows) + shift
                    gathered[q, step, rows, :] = gelu_tanh(pre).astype(jnp.bfloat16)

                in_rows(body)

            @pl.when(step >= parts)
            def _():
                def body(rows):
                    pre = total_of(step - parts, rows) + shift
                    slope = total_of(step, rows) * gelu_slope(pre)
                    gathered[q, step, rows, :] = slope.astype(jnp.bfloat16)

                in_rows(body)

            ring_copy(way, step).start()
            hand_copy(way, step, q).start()

    def pass_on(way, step, hop):
        ring_copy(way, step).wait_recv()

        @pl.when(hop > 0)
        def _():
            ring_copy(way, step).start()

        hand_copy(way, step, way * 2 + core).start()

    def within(step):
        return jnp.logical_and(step >= 0, step < steps)

    def both_kinds(step, act):
        @pl.when(step < parts)
        def _():
            act(True)

        @pl.when(step >= parts)
        def _():
            act(False)

    def turn(now, carry):
        @pl.when(now < steps)
        def _():
            def start(item, inner):
                both_kinds(now, lambda first: near_copy(item, now, first).start())
                return inner

            lax.fori_loop(0, 4, start, 0)

        for way in range(2):
            used = now - 2 - 2 * (length - 1) + hops(way)

            @pl.when(within(used))
            def _(way=way, used=used):
                for which in range(2):
                    both_kinds(used, lambda first: far_copy(way, which, used, not first).start())

        for way in range(2):
            hop = hops(way)
            ready = now - 1 - hop

            @pl.when(within(ready))
            def _(way=way, ready=ready, hop=hop):
                combine(way, ready, hop)

        @pl.when(now == parts)
        def _():
            shared(1)

        @pl.when(now < steps)
        def _():
            def one(item, inner):
                way, own, _ = near_quarter(item)
                slot = jnp.where(own == 1, now, steps + now % 2)

                @pl.when(jnp.logical_and(own == 0, now >= 2))
                def _():
                    pair_copy(way, now).wait_send()

                @pl.when(now < parts)
                def _():
                    near_copy(item, now, True).wait()
                    mine[way, slot] = times(tok[...], near_in[item]).astype(jnp.bfloat16)

                @pl.when(now >= parts)
                def _():
                    near_copy(item, now, False).wait()
                    mine[way, slot] = times_transposed(cot[...], near_out[item]).astype(jnp.bfloat16)

                @pl.when(own == 0)
                def _():
                    pair_copy(way, now).start()

                return inner

            lax.fori_loop(0, 4, one, 0)

        for way in range(2):
            hop = hops(way)
            here = now - 1 - 2 * (length - 1) + hop

            @pl.when(jnp.logical_and(within(here), hop < length - 1))
            def _(way=way, here=here, hop=hop):
                pass_on(way, here, hop)

        def use(way, inner):
            hop = jnp.where(way == 0, hops(0), hops(1))
            used = now - 2 - 2 * (length - 1) + hop

            @pl.when(within(used))
            def _():
                hand_copy(way, used, way * 2 + 1 - core).wait_recv()
                for which in range(2):
                    both_kinds(used, lambda first: store_copy(way * 2 + which, used, first).start())
                slab = depth // 3

                @pl.when(used < parts)
                def _():
                    for which in range(2):
                        far_copy(way, which, used, False).wait()
                    for third in range(3):
                        at = slice(third * slab, (third + 1) * slab)
                        acc_o[:, at] += times(gathered[way * 2, used], far_out[way * 2, :, at]) + times(
                            gathered[way * 2 + 1, used], far_out[way * 2 + 1, :, at])

                @pl.when(used >= parts)
                def _():
                    for which in range(2):
                        far_copy(way, which, used, True).wait()
                    for third in range(3):
                        at = slice(third * slab, (third + 1) * slab)
                        acc_g[:, at] += times_transposed(
                            gathered[way * 2, used], far_in[way * 2, at, :]
                        ) + times_transposed(gathered[way * 2 + 1, used], far_in[way * 2 + 1, at, :])

            return inner

        lax.fori_loop(0, 2, use, 0)

        @pl.when(now == parts - 1 + 2 * length)
        def _():
            staged[...] = acc_o[...].astype(jnp.bfloat16)
            for offset in range(1, groups):
                out_copy(offset).start()

        return carry

    lax.fori_loop(0, steps + 2 * length, turn, 0)
    for offset in range(1, groups):
        out_copy(offset).wait_recv()
    total = acc_o[rows_of(group), :]
    for offset in range(1, groups):
        total = total + landed[offset - 1].astype(jnp.float32)
    out_o[...] = total.astype(jnp.bfloat16)
    gt_o[...] = acc_g[...].astype(jnp.bfloat16)

    def finish(step, carry):
        for way in range(2):
            hop = hops(way)

            @pl.when(hop < length - 1)
            def _(way=way):
                sum_copy(way, step).wait_send()

            @pl.when(hop > 0)
            def _(way=way):
                ring_copy(way, step).wait_send()

            hand_copy(way, step, way * 2 + core).wait_send()
            for which in range(2):
                both_kinds(step, lambda first: store_copy(way * 2 + which, step, first).wait())
        return carry

    lax.fori_loop(0, steps, finish, 0)
    for kind in range(2):
        whole_copy(kind).wait()
        for offset in range(1, groups):
            share_copy(kind, offset, group).wait_send()
    for offset in range(1, groups):
        out_copy(offset).wait_send()
    for way in range(2):
        for step in (steps - 2, steps - 1):
            pair_copy(way, step).wait_send()


def chain(length, groups, tokens, cotangent, bias_wide, weight_in, weight_out):
    rows_each, depth = tokens.shape
    count = rows_each * groups
    hidden_units = weight_in.shape[1]
    parts = hidden_units // (4 * wide)
    steps = 2 * parts
    bf16 = jnp.bfloat16
    vmem = pl.BlockSpec(memory_space=pltpu.VMEM)
    anywhere = pl.BlockSpec(memory_space=pl.ANY)
    dma = pltpu.SemaphoreType.DMA
    return pl.pallas_call(
        functools.partial(chain_kernel, length, groups, parts),
        out_shape=(
            jax.ShapeDtypeStruct((count, hidden_units), bf16),
            jax.ShapeDtypeStruct((count, hidden_units), bf16),
            jax.ShapeDtypeStruct((rows_each, depth), bf16),
            jax.ShapeDtypeStruct((count, depth), bf16),
            jax.ShapeDtypeStruct((count, depth), bf16),
            jax.ShapeDtypeStruct((count, depth), bf16),
        ),
        in_specs=[anywhere, anywhere, vmem, anywhere, anywhere],
        out_specs=(anywhere, anywhere, vmem, vmem, anywhere, anywhere),
        scratch_shapes=[
            pltpu.VMEM((count, depth), bf16),
            pltpu.VMEM((count, depth), bf16),
            pltpu.VMEM((count, depth), bf16),
            pltpu.VMEM((groups - 1, rows_each, depth), bf16),
            pltpu.VMEM((4, steps, count, wide), bf16),
            pltpu.VMEM((2, steps, count, wide), bf16),
            pltpu.VMEM((2, steps, count, wide), bf16),
            pltpu.VMEM((2, steps + 2, count, wide), bf16),
            pltpu.VMEM((4, depth, wide), bf16),
            pltpu.VMEM((4, wide, depth), bf16),
            pltpu.VMEM((4, depth, wide), bf16),
            pltpu.VMEM((4, wide, depth), bf16),
            pltpu.VMEM((count, depth), jnp.float32),
            pltpu.VMEM((count, depth), jnp.float32),
            dma((2, steps)), dma((2, steps)), dma((2, 2)), dma((2, steps)),
            dma((2, steps)), dma((2, steps)), dma((2, steps)), dma((2, steps)),
            dma((4,)), dma((4,)), dma((4, steps)),
            dma((2,)), dma((2,)), dma((2, groups)), dma((2, groups)), dma((groups,)), dma((groups,)),
        ],
        compiler_params=pltpu.CompilerParams(
            collective_id=0, has_side_effects=True, vmem_limit_bytes=61 * 1024 * 1024
        ),
    )(tokens, cotangent, bias_wide.reshape(-1, 1, wide), weight_in, weight_out)


def slope_kernel(factor, left, right, grad, total, turned):
    @pl.when(pl.program_id(0) == 0)
    def _():
        turned[...] = left[...].T

    grad[...] = (times(turned[...], right[...]) * factor).astype(jnp.bfloat16)
    total[...] = jnp.sum(right[...].astype(jnp.float32), axis=0, keepdims=True) * factor


def slope_grads(factor, left, right):
    count, depth = left.shape
    units = right.shape[1]
    block = 2 * wide
    return pl.pallas_call(
        functools.partial(slope_kernel, factor),
        grid=(units // block,),
        out_shape=(
            jax.ShapeDtypeStruct((depth, units), jnp.bfloat16),
            jax.ShapeDtypeStruct((1, units), jnp.float32),
        ),
        in_specs=[
            pl.BlockSpec((count, depth), lambda j: (0, 0)),
            pl.BlockSpec((count, block), lambda j: (0, j)),
        ],
        out_specs=(
            pl.BlockSpec((depth, block), lambda j: (0, j)),
            pl.BlockSpec((1, block), lambda j: (0, j)),
        ),
        scratch_shapes=[pltpu.VMEM((depth, count), jnp.bfloat16)],
        compiler_params=pltpu.CompilerParams(vmem_limit_bytes=60 * 1024 * 1024),
        cost_estimate=pl.CostEstimate(
            flops=2 * count * depth * units,
            bytes_accessed=2 * (count * depth + count * units + depth * units),
            transcendentals=0,
        ),
    )(left, right)


def hidden_kernel(factor, left, right, grad):
    grad[...] = (times(left[...].T, right[...]) * factor).astype(jnp.bfloat16)


def hidden_grads(factor, left, right):
    count, units = left.shape
    depth = right.shape[1]
    block = 2 * wide
    return pl.pallas_call(
        functools.partial(hidden_kernel, factor),
        grid=(units // block,),
        out_shape=jax.ShapeDtypeStruct((units, depth), jnp.bfloat16),
        in_specs=[
            pl.BlockSpec((count, block), lambda j: (0, j)),
            pl.BlockSpec((count, depth), lambda j: (0, 0)),
        ],
        out_specs=pl.BlockSpec((block, depth), lambda j: (j, 0)),
        compiler_params=pltpu.CompilerParams(vmem_limit_bytes=60 * 1024 * 1024),
        cost_estimate=pl.CostEstimate(
            flops=2 * count * depth * units,
            bytes_accessed=2 * (count * depth + count * units + depth * units),
            transcendentals=0,
        ),
    )(left, right)


def per_device(length, groups, tokens, weight_in, weight_out, bias_in, cotangent):
    rows_here = tokens.shape[0]
    total_rows = rows_here * lax.axis_size("col")
    factor = 1.0 / math.sqrt(total_rows)
    hidden_all, slope_all, output, grad_tokens, tokens_all, cotangent_all = chain(
        length, groups, tokens, cotangent, bias_in.astype(jnp.float32), weight_in, weight_out
    )
    grad_tokens = lax.psum_scatter(grad_tokens, "col", scatter_dimension=0, tiled=True)
    grad_weight_out = hidden_grads(factor, hidden_all, cotangent_all)
    grad_weight_in, grad_bias = slope_grads(factor, tokens_all, slope_all)
    grad_bias = grad_bias.reshape(-1)
    return (output, grad_tokens, grad_weight_in, grad_weight_out, grad_bias)


def solution(mesh):
    placed = (P("col", "row"), P("row", "col"), P("col", "row"), P("col"), P("col", "row"))
    return jax.shard_map(
        functools.partial(per_device, mesh.shape["row"] // 2, mesh.shape["col"]),
        mesh=mesh,
        in_specs=placed,
        out_specs=(P("col", "row"), P("col", "row"), P("row", "col"), P("col", "row"), P("col")),
        check_vma=False,
    )
```
